512 devices in a mesh: col: 16 (over x, z_hi, core), row: 32 (over y, z_lo).
Axes of the slice: x: 4, y: 8, z: 8 (z_hi: 2, z_lo: 4; z = z_hi * 4 + z_lo), core: 2. Of those that a mesh axis runs over, the one named last changes fastest.
Arguments:
- features: bfloat16 [131072, 256], P(('col', 'row')), may hold values from -6 to 6
- tiles: bfloat16 [32768, 128, 128], P(('col', 'row')), as said below
- tile_dst: int32 [32768], P(('col', 'row')), may hold values from 0 to 63
- tile_src: int32 [32768], P(('col', 'row')), may hold values from 0 to 1
- weight: bfloat16 [256, 256], replicated, may hold values from -0.375 to 0.375
- bias: float32 [256], replicated, may hold values from -3 to 3
Outputs:
- activated: bfloat16 [131072, 256], P(('col', 'row'))
The draws below stay inside these ranges and needn't reach their ends.
Inputs may be any that keep to these rules, and one draw needn't show every extreme that they name: `tiles`: entries are zero or positive edge weights; about one in 32 entries of a tile is nonzero.
All inputs are finite; a program needn't handle non-finite values.
Results may differ from the reference program's by a relative error of at most 0.022.
Values may be sent and summed in bfloat16 or wider, within the bound.
No kernel may reach another device: no remote copies, remote signals or barrier semaphores. Data moves between devices by JAX's collectives and lax.ppermute only.
A program may use at most 64 MiB of HBM per device.

```python
import math
import jax
import jax.numpy as jnp
import numpy as np
from jax import lax

HID = 256
TILE = 128
TD = 64
SB_DEV = 2
WINDOW = 64
NB_DST = 1024
TILES_ALL = 32768
NODES = 131072
N_COL = 16
N_ROW = 32


def draw_tiles(key, part):
    key = jax.random.fold_in(key, 7)
    mask_key, value_key = jax.random.split(key, 2)
    shape = (TILES_ALL, TILE, TILE)
    density = 1.0 / 32.0
    expected = TD / SB_DEV * TILE * density
    present = jax.random.uniform(mask_key, shape, jnp.float32) < density
    values = jax.random.uniform(value_key, shape, jnp.float32, 0.5, 1.5)
    return (jnp.where(present, values, 0.0) / jnp.sqrt(expected)).astype(jnp.bfloat16)


def place_ends(result, rng, least, largest):
    spot = [jax.random.randint(jax.random.fold_in(rng, axis), (), 0, length) for axis, length in enumerate(result.shape)]
    widest = result.shape.index(max(result.shape))
    next_to = spot[:widest] + [(spot[widest] + 1) % result.shape[widest]] + spot[widest + 1:]
    return result.at[tuple(spot)].set(least).at[tuple(next_to)].set(largest)


def block_levels(key, shape, cuts, smallest, largest):
    def one(position, shards_of):
        heights = jax.random.uniform(jax.random.fold_in(jax.random.fold_in(key, 6), position), (shards_of,), jnp.float32, smallest / len(cuts), largest / len(cuts))
        return jnp.repeat(jnp.exp(heights), shape[position] // shards_of).reshape((-1,) + (1,) * (len(shape) - position - 1))

    level = one(*cuts[0])
    for cut in cuts[1:]:
        level = level * one(*cut)
    return level


def rank_bounds(amount, slope):
    loads = [(1 << 20) // math.isqrt(standing ** slope) + 1 for standing in range(1, amount + 1)]
    scale = 1 + sum(loads) // (1 << 30)
    return np.cumsum(np.array([max(1, weight // scale) for weight in loads]))


def ranked_ids(own_key, dims, count, skew):
    table = rank_bounds(count, skew)
    pick = jax.random.randint(jax.random.fold_in(own_key, 1), dims, 0, int(table[count - 1]))
    grade = jnp.searchsorted(jnp.asarray(table, jnp.int32), pick, side="right")
    return jax.random.permutation(jax.random.fold_in(own_key, 2), count)[grade].astype(jnp.int32)


def bell_draw(rng, extent, deviation, bound, shards=(), kind=jnp.bfloat16):
    drawn = deviation * jax.random.normal(rng, extent, jnp.float32)
    if shards:
        drawn = drawn * block_levels(rng, extent, shards, -0.22, 0.18)
    return jnp.clip(drawn, -bound, bound).astype(kind)


def setup_inputs(seed: int = 0) -> dict:
    keys = jax.random.split(jax.random.key(seed), 7)
    return {
        "features": bell_draw(keys[0], (NODES, HID), 1.0, 6.0, ((0, 512),)),
        "tiles": draw_tiles(jax.random.fold_in(keys[6], 71), 0),
        "tile_dst": place_ends(ranked_ids(keys[2], (TILES_ALL,), WINDOW, 1), jax.random.fold_in(keys[2], 3), 0, WINDOW - 1).astype(jnp.int32),
        "tile_src": place_ends(jax.random.randint(keys[3], (TILES_ALL,), 0, SB_DEV), jax.random.fold_in(keys[3], 1), 0, SB_DEV - 1).astype(jnp.int32),
        "weight": bell_draw(keys[4], (HID, HID), HID ** -0.5, 0.375),
        "bias": bell_draw(keys[5], (HID,), 0.5, 3.0, (), jnp.float32),
    }


def reference(features, tiles, tile_dst, tile_src, weight, bias):
    groups = N_COL * N_ROW
    window_count = 2 * N_COL * SB_DEV
    blocks_x = features.reshape(groups, SB_DEV, TILE, HID)
    blocks_t = tiles.reshape(groups, TD, TILE, TILE)
    dst_all = tile_dst.reshape(groups, TD).astype(jnp.int32)
    src_all = tile_src.reshape(groups, TD).astype(jnp.int32)
    windows = jnp.arange(window_count, dtype=jnp.int32)
    col_part = windows // (2 * SB_DEV)
    half_part = (windows // SB_DEV) % 2
    local_part = windows % SB_DEV
    group_ids = jnp.arange(groups, dtype=jnp.int32)

    def one_group(total, inputs):
        group_id, tile_group, dst_group, src_group, block_group = inputs
        picked = block_group[src_group]
        prods = jnp.einsum("tij,tjh->tih", tile_group.astype(jnp.float32), picked.astype(jnp.float32))
        part = jax.ops.segment_sum(prods, dst_group, num_segments=window_count)
        part = lax.optimization_barrier(part.astype(jnp.bfloat16)).astype(jnp.float32)
        row_here = group_id % N_ROW
        target = ((col_part * N_ROW + (row_here + half_part) % N_ROW) * SB_DEV + local_part).astype(jnp.int32)
        return total.at[target].add(part), None

    start = jnp.zeros((NB_DST, TILE, HID), jnp.float32)
    summed, _ = lax.scan(one_group, start, (group_ids, blocks_t, dst_all, src_all, blocks_x))
    aggregate_b = summed.reshape(NB_DST * TILE, HID).astype(jnp.bfloat16)
    mixed = jnp.dot(aggregate_b, weight, preferred_element_type=jnp.float32) + bias
    return jnp.maximum(mixed, 0.0).astype(jnp.bfloat16)
```

```python
import jax
import jax.numpy as jnp
from jax import lax
from jax.experimental import pallas as pl
from jax.experimental.pallas import tpu as pltpu
from jax.sharding import PartitionSpec as P

N_X, N_HI, N_CORE, N_ROW = 4, 2, 2, 32
AXES = ("col", "row")
GROUP = 8


def route(move):
    pairs = []
    for c in range(N_X * N_HI * N_CORE):
        for r in range(N_ROW):
            x, hi, core, row = move(c // 4, (c // 2) % 2, c % 2, r)
            target = ((x % N_X) * 4 + hi * 2 + core) * N_ROW + row % N_ROW
            pairs.append((c * N_ROW + r, target))
    return pairs


def send(block, move):
    return lax.ppermute(block, AXES, route(move))


def chip_sums(meta, dst_a, src_a, dst_b, src_b, tiles_a, tiles_b, feats_a, feats_b):
    count, size, _ = tiles_a.shape
    width = feats_a.shape[-1]

    def kernel(meta, dst_a, src_a, dst_b, src_b, tiles_a, tiles_b, feats_a, feats_b, *rest):
        outs, acc, todo = rest[:N_X], rest[N_X], rest[N_X + 1]
        x_here, wanted = meta[0], meta[1]
        acc[...] = jnp.zeros_like(acc)

        def run(dst, src, tiles, feats):
            def scan(i, n):
                slot = dst[i]
                place = (((slot >> 4) - x_here) & 3) * 4 + (slot & 3)
                todo[n] = i | (src[i] << 8) | (place << 16)
                return n + (((slot >> 2) & 3) == wanted).astype(jnp.int32)

            n = lax.fori_loop(0, count, scan, 0, unroll=8)
            for j in range(GROUP - 1):
                todo[n + j] = 16 << 16

            def add(g, carry):
                items = [todo[g * GROUP + j] for j in range(GROUP)]
                prods = [
                    jnp.dot(tiles[e & 255], feats[(e >> 8) & 255], preferred_element_type=jnp.float32)
                    for e in items
                ]
                for e, prod in zip(items, prods):
                    acc[e >> 16] += prod
                return carry

            lax.fori_loop(0, (n + GROUP - 1) // GROUP, add, 0)

        run(dst_a, src_a, tiles_a, feats_a)
        run(dst_b, src_b, tiles_b, feats_b)
        for d, out in enumerate(outs):
            out[...] = acc[4 * d : 4 * d + 4].reshape(4 * size, width).astype(out.dtype)

    smem = pl.BlockSpec(memory_space=pltpu.SMEM)
    vmem = pl.BlockSpec(memory_space=pltpu.VMEM)
    return pl.pallas_call(
        kernel,
        out_shape=[jax.ShapeDtypeStruct((4 * size, width), jnp.bfloat16)] * N_X,
        in_specs=[smem] * 5 + [vmem] * 4,
        out_specs=[vmem] * N_X,
        scratch_shapes=[pltpu.VMEM((17, size, width), jnp.float32), pltpu.SMEM((count + GROUP,), jnp.int32)],
        compiler_params=pltpu.CompilerParams(vmem_limit_bytes=32 * 2**20),
        cost_estimate=pl.CostEstimate(flops=32 * 2 * size * size * width, bytes_accessed=7 * 2**20, transcendentals=0),
    )(meta, dst_a, src_a, dst_b, src_b, tiles_a, tiles_b, feats_a, feats_b)


def over_x(parts):
    far = send(parts[2], lambda x, hi, core, row: (x + 2, hi, core, row))
    right = send(parts[1], lambda x, hi, core, row: (x + 1, hi, core, row))
    left = send(parts[3], lambda x, hi, core, row: (x - 1, hi, core, row))
    return [parts[0], right, left, far]


def total(parts):
    result = parts[0].astype(jnp.float32)
    for part in parts[1:]:
        result = result + part.astype(jnp.float32)
    return result


def shards(features, tiles, tile_dst, tile_src, weight, bias):
    count, size, _ = tiles.shape
    width = features.shape[1]
    blocks = features.shape[0] // size
    col = lax.axis_index("col")
    x_here, hi_here, core_here = col // 4, (col // 2) % 2, col % 2

    def other_core(block):
        return send(block, lambda x, hi, core, row: (x, hi, 1 - core, row))

    their_tiles = other_core(tiles)
    slots = jnp.zeros((16, width), jnp.bfloat16)
    slots = slots.at[0, :count].set(tile_dst.astype(jnp.bfloat16)).at[1, :count].set(tile_src.astype(jnp.bfloat16))
    theirs = other_core(jnp.concatenate([features, slots], axis=0))
    their_feats = theirs[: blocks * size]
    their_dst = theirs[blocks * size, :count].astype(jnp.int32)
    their_src = theirs[blocks * size + 1, :count].astype(jnp.int32)

    def sums_for(hi):
        meta = jnp.stack([x_here, hi * 2 + core_here]).astype(jnp.int32)
        return chip_sums(
            meta, tile_dst, tile_src, their_dst, their_src, tiles, their_tiles,
            features.reshape(blocks, size, width), their_feats.reshape(blocks, size, width),
        )

    half = blocks * size
    away = over_x(sums_for(1 - hi_here))
    home = over_x(sums_for(hi_here))
    away_sum = total(away).astype(jnp.bfloat16)
    same_row = send(away_sum[:half], lambda x, hi, core, row: (x, 1 - hi, core, row))
    next_row = send(away_sum[half:], lambda x, hi, core, row: (x, 1 - hi, core, row + 1))
    passed = total([part[half:] for part in home]).astype(jnp.bfloat16)
    passed = send(passed, lambda x, hi, core, row: (x, hi, core, row + 1))
    aggregate = total([part[:half] for part in home] + [same_row, next_row, passed])
    mixed = jnp.dot(aggregate.astype(jnp.bfloat16), weight, preferred_element_type=jnp.float32) + bias
    return jnp.maximum(mixed, 0.0).astype(jnp.bfloat16)


def solution(mesh):
    in_specs = (
        P(("col", "row"), None),
        P(("col", "row"), None, None),
        P(("col", "row")),
        P(("col", "row")),
        P(),
        P(),
    )
    out_specs = P(("col", "row"), None)
    return jax.shard_map(shards, mesh=mesh, in_specs=in_specs, out_specs=out_specs, check_vma=False)
```

```python
import jax
import jax.numpy as jnp
from jax import lax
from jax.experimental import pallas as pl
from jax.experimental.pallas import tpu as pltpu
from jax.sharding import PartitionSpec as P

N_X, N_HI, N_CORE, N_ROW = 4, 2, 2, 32
AXES = ("col", "row")
GROUP = 8
LOADS = 4


def route(move):
    pairs = []
    for c in range(N_X * N_HI * N_CORE):
        for r in range(N_ROW):
            x, hi, core, row = move(c // 4, (c // 2) % 2, c % 2, r)
            target = ((x % N_X) * 4 + hi * 2 + core) * N_ROW + row % N_ROW
            pairs.append((c * N_ROW + r, target))
    return pairs


def send(block, move):
    return lax.ppermute(block, AXES, route(move))


def half_sums(wanted, features, tiles, tile_dst, tile_src):
    count, size, _ = tiles.shape
    width = features.shape[-1]
    places = N_HI * N_X * 2 * 2
    load = count // LOADS

    def kernel(meta, dst_in, src_in, tiles_in, feats_in, out, acc, held, feats, dst, src, todo, sems):
        copies = [
            pltpu.make_async_copy(dst_in, dst, sems.at[LOADS]),
            pltpu.make_async_copy(src_in, src, sems.at[LOADS + 1]),
            pltpu.make_async_copy(feats_in, feats, sems.at[LOADS + 2]),
        ]
        loads = [
            pltpu.make_async_copy(tiles_in.at[pl.ds(i * load, load)], held.at[pl.ds(i * load, load)], sems.at[i])
            for i in range(LOADS)
        ]
        for copy in copies + loads:
            copy.start()
        x_here, hi_here, core = meta[0], meta[1], meta[2]
        acc[...] = jnp.zeros_like(acc)
        copies[0].wait()
        copies[1].wait()

        def scan(i, n):
            slot = dst[i]
            near = 1 - (((slot >> 3) & 1) ^ hi_here)
            place = near * 16 + (((slot >> 4) - x_here) & 3) * 4 + (slot & 3)
            todo[n] = i | (src[i] << 8) | (place << 16)
            return n + (((slot >> 2) & 1) == core).astype(jnp.int32)

        ends = []
        n = jnp.int32(0)
        for i in range(LOADS):
            n = lax.fori_loop(i * load, (i + 1) * load, scan, n, unroll=8)
            ends.append(n // GROUP)
        for j in range(GROUP - 1):
            todo[n + j] = places << 16
        ends[-1] = (n + GROUP - 1) // GROUP

        def add(g, carry):
            items = [todo[g * GROUP + j] for j in range(GROUP)]
            prods = [
                jnp.dot(held[e & 255], feats[(e >> 8) & 255], preferred_element_type=jnp.float32) for e in items
            ]
            for e, prod in zip(items, prods):
                acc[e >> 16] += prod
            return carry

        copies[2].wait()
        begin = jnp.int32(0)
        for i in range(LOADS):
            loads[i].wait()
            lax.fori_loop(begin, ends[i], add, 0)
            begin = ends[i]
        out[...] = acc[:places].astype(out.dtype)

    smem = pl.BlockSpec(memory_space=pltpu.SMEM)
    hbm = pl.BlockSpec(memory_space=pltpu.HBM)
    col = lax.axis_index("col")
    meta = jnp.stack([col >> 2, (col >> 1) & 1, wanted(col & 1)]).astype(jnp.int32)
    operands = [tile_dst, tile_src, tiles, features.reshape(-1, size, width)]
    operands = [pltpu.with_memory_space_constraint(operand, pltpu.HBM) for operand in operands]
    return pl.pallas_call(
        kernel,
        out_shape=jax.ShapeDtypeStruct((places, size, width), jnp.bfloat16),
        in_specs=[smem] + [hbm] * 4,
        out_specs=pl.BlockSpec(memory_space=pltpu.VMEM),
        scratch_shapes=[
            pltpu.VMEM((places + 1, size, width), jnp.float32),
            pltpu.VMEM(tiles.shape, tiles.dtype),
            pltpu.VMEM((features.shape[0] // size, size, width), features.dtype),
            pltpu.SMEM((count,), jnp.int32),
            pltpu.SMEM((count,), jnp.int32),
            pltpu.SMEM((count + GROUP,), jnp.int32),
            pltpu.SemaphoreType.DMA((LOADS + 3,)),
        ],
        compiler_params=pltpu.CompilerParams(vmem_limit_bytes=32 * 2**20),
        cost_estimate=pl.CostEstimate(flops=32 * 2 * size * size * width, bytes_accessed=5 * 2**20, transcendentals=0),
    )(meta, *operands)


def total(parts):
    result = parts[0].astype(jnp.float32)
    for part in parts[1:]:
        result = result + part.astype(jnp.float32)
    return result


def shards(features, tiles, tile_dst, tile_src, weight, bias):
    size = tiles.shape[1]
    width = features.shape[1]
    operands = (features, tiles, tile_dst, tile_src)
    theirs = half_sums(lambda core: 1 - core, *operands)
    arrived = send(theirs, lambda x, hi, core, row: (x, hi, 1 - core, row))
    mine = half_sums(lambda core: core, *operands)

    def both(first, n):
        return total([mine[first : first + n], arrived[first : first + n]]).astype(jnp.bfloat16)

    def pieces_of(first):
        return lax.optimization_barrier([both(first + 4 * d, 4) for d in range(N_X)])

    def over_x(pieces, order):
        got = [send(pieces[d], lambda x, hi, core, row, d=d: (x + d, hi, core, row)) for d in order]
        return [pieces[0]] + got

    for_away, for_home = pieces_of(0), pieces_of(16)
    away = total(over_x(for_away, (2, 1, 3))).astype(jnp.bfloat16)
    home = over_x(for_home, (1, 3, 2))
    same_row = send(away[:2], lambda x, hi, core, row: (x, 1 - hi, core, row))
    next_row = send(away[2:], lambda x, hi, core, row: (x, 1 - hi, core, row + 1))
    passed = total([part[2:] for part in home]).astype(jnp.bfloat16)
    passed = send(passed, lambda x, hi, core, row: (x, hi, core, row + 1))
    last = [part[:2] for part in home] + [same_row, next_row, passed]
    aggregate = total(last).reshape(2 * size, width)
    mixed = jnp.dot(aggregate.astype(jnp.bfloat16), weight, preferred_element_type=jnp.float32) + bias
    return jnp.maximum(mixed, 0.0).astype(jnp.bfloat16)


def solution(mesh):
    in_specs = (
        P(("col", "row"), None),
        P(("col", "row"), None, None),
        P(("col", "row")),
        P(("col", "row")),
        P(),
        P(),
    )
    out_specs = P(("col", "row"), None)
    return jax.shard_map(shards, mesh=mesh, in_specs=in_specs, out_specs=out_specs, check_vma=False)
```

```python
import jax
import jax.numpy as jnp
from jax import lax
from jax.experimental import pallas as pl
from jax.experimental.pallas import tpu as pltpu
from jax.sharding import PartitionSpec as P

N_X, N_HI, N_CORE, N_ROW = 4, 2, 2, 32
AXES = ("col", "row")
GROUP = 8
LOADS = 4


def route(move):
    pairs = []
    for c in range(N_X * N_HI * N_CORE):
        for r in range(N_ROW):
            x, hi, core, row = move(c // 4, (c // 2) % 2, c % 2, r)
            target = ((x % N_X) * 4 + hi * 2 + core) * N_ROW + row % N_ROW
            pairs.append((c * N_ROW + r, target))
    return pairs


def send(block, move):
    return lax.ppermute(block, AXES, route(move))


def half_sums(wanted, features, tiles, tile_dst, tile_src):
    count, size, _ = tiles.shape
    width = features.shape[-1]
    places = N_HI * N_X * 2 * 2
    load = count // LOADS

    def kernel(meta, dst_in, src_in, tiles_in, feats_in, out, acc, held, feats, dst, src, todo, sems):
        copies = [
            pltpu.make_async_copy(dst_in, dst, sems.at[LOADS]),
            pltpu.make_async_copy(src_in, src, sems.at[LOADS + 1]),
            pltpu.make_async_copy(feats_in, feats, sems.at[LOADS + 2]),
        ]
        loads = [
            pltpu.make_async_copy(tiles_in.at[pl.ds(i * load, load)], held.at[pl.ds(i * load, load)], sems.at[i])
            for i in range(LOADS)
        ]
        for copy in copies + loads:
            copy.start()
        x_here, hi_here, core = meta[0], meta[1], meta[2]
        acc[...] = jnp.zeros_like(acc)
        copies[0].wait()
        copies[1].wait()

        def scan(i, n):
            slot = dst[i]
            near = 1 - (((slot >> 3) & 1) ^ hi_here)
            place = near * 16 + (((slot >> 4) ^ x_here) & 3) * 4 + (slot & 3)
            todo[n] = i | (src[i] << 8) | (place << 16)
            return n + (((slot >> 2) & 1) == core).astype(jnp.int32)

        ends = []
        n = jnp.int32(0)
        for i in range(LOADS):
            n = lax.fori_loop(i * load, (i + 1) * load, scan, n, unroll=8)
            ends.append(n // GROUP)
        for j in range(GROUP - 1):
            todo[n + j] = places << 16
        ends[-1] = (n + GROUP - 1) // GROUP

        def add(g, carry):
            items = [todo[g * GROUP + j] for j in range(GROUP)]
            prods = [
                jnp.dot(held[e & 255], feats[(e >> 8) & 255], preferred_element_type=jnp.float32) for e in items
            ]
            for e, prod in zip(items, prods):
                acc[e >> 16] += prod
            return carry

        copies[2].wait()
        begin = jnp.int32(0)
        for i in range(LOADS):
            loads[i].wait()
            lax.fori_loop(begin, ends[i], add, 0)
            begin = ends[i]
        out[...] = acc[:places].astype(out.dtype)

    smem = pl.BlockSpec(memory_space=pltpu.SMEM)
    hbm = pl.BlockSpec(memory_space=pltpu.HBM)
    col = lax.axis_index("col")
    meta = jnp.stack([col >> 2, (col >> 1) & 1, wanted(col & 1)]).astype(jnp.int32)
    operands = [tile_dst, tile_src, tiles, features.reshape(-1, size, width)]
    operands = [pltpu.with_memory_space_constraint(operand, pltpu.HBM) for operand in operands]
    return pl.pallas_call(
        kernel,
        out_shape=jax.ShapeDtypeStruct((places, size, width), jnp.bfloat16),
        in_specs=[smem] + [hbm] * 4,
        out_specs=pl.BlockSpec(memory_space=pltpu.VMEM),
        scratch_shapes=[
            pltpu.VMEM((places + 1, size, width), jnp.float32),
            pltpu.VMEM(tiles.shape, tiles.dtype),
            pltpu.VMEM((features.shape[0] // size, size, width), features.dtype),
            pltpu.SMEM((count,), jnp.int32),
            pltpu.SMEM((count,), jnp.int32),
            pltpu.SMEM((count + GROUP,), jnp.int32),
            pltpu.SemaphoreType.DMA((LOADS + 3,)),
        ],
        compiler_params=pltpu.CompilerParams(vmem_limit_bytes=32 * 2**20),
        cost_estimate=pl.CostEstimate(flops=32 * 2 * size * size * width, bytes_accessed=5 * 2**20, transcendentals=0),
    )(meta, *operands)


def total(parts):
    result = parts[0].astype(jnp.float32)
    for part in parts[1:]:
        result = result + part.astype(jnp.float32)
    return result


def shards(features, tiles, tile_dst, tile_src, weight, bias):
    size = tiles.shape[1]
    width = features.shape[1]
    operands = (features, tiles, tile_dst, tile_src)
    theirs = half_sums(lambda core: 1 - core, *operands)
    arrived = send(theirs, lambda x, hi, core, row: (x, hi, 1 - core, row))
    mine = half_sums(lambda core: core, *operands)

    def both(first, n):
        return total([mine[first : first + n], arrived[first : first + n]]).astype(jnp.bfloat16)

    def pieces_of(first):
        return lax.optimization_barrier([both(first + 4 * d, 4) for d in range(N_X)])

    def over_x(pieces, order):
        got = [send(pieces[d], lambda x, hi, core, row, d=d: (x ^ d, hi, core, row)) for d in order]
        return [pieces[0]] + got

    for_away = pieces_of(0)
    for_away, arrived, mine = lax.optimization_barrier((for_away, arrived, mine))
    for_home = pieces_of(16)
    away = total(over_x(for_away, (2, 3, 1))).astype(jnp.bfloat16)
    home = over_x(for_home, (3, 1, 2))
    same_row = send(away[:2], lambda x, hi, core, row: (x, 1 - hi, core, row))
    next_row = send(away[2:], lambda x, hi, core, row: (x, 1 - hi, core, row + 1))
    passed = total([part[2:] for part in home]).astype(jnp.bfloat16)
    passed = send(passed, lambda x, hi, core, row: (x, hi, core, row + 1))
    last = [part[:2] for part in home] + [same_row, next_row, passed]
    aggregate = total(last).reshape(2 * size, width)
    mixed = jnp.dot(aggregate.astype(jnp.bfloat16), weight, preferred_element_type=jnp.float32) + bias
    return jnp.maximum(mixed, 0.0).astype(jnp.bfloat16)


def solution(mesh):
    in_specs = (
        P(("col", "row"), None),
        P(("col", "row"), None, None),
        P(("col", "row")),
        P(("col", "row")),
        P(),
        P(),
    )
    out_specs = P(("col", "row"), None)
    return jax.shard_map(shards, mesh=mesh, in_specs=in_specs, out_specs=out_specs, check_vma=False)
```

```python
import jax
import jax.numpy as jnp
from jax import lax
from jax.experimental import pallas as pl
from jax.experimental.pallas import tpu as pltpu
from jax.sharding import PartitionSpec as P

N_X, N_HI, N_CORE, N_ROW = 4, 2, 2, 32
AXES = ("col", "row")
GROUP = 16
LOADS = 4


def route(move):
    pairs = []
    for c in range(N_X * N_HI * N_CORE):
        for r in range(N_ROW):
            x, hi, core, row = move(c // 4, (c // 2) % 2, c % 2, r)
            target = ((x % N_X) * 4 + hi * 2 + core) * N_ROW + row % N_ROW
            pairs.append((c * N_ROW + r, target))
    return pairs


def send(block, move):
    return lax.ppermute(block, AXES, route(move))


def half_sums(wanted, features, tiles, tile_dst, tile_src):
    count, size, _ = tiles.shape
    width = features.shape[-1]
    places = N_HI * N_X * 2 * 2
    load = count // LOADS

    def kernel(meta, dst_in, src_in, tiles_in, feats_in, out, acc, held, feats, dst, src, todo, sems):
        copies = [
            pltpu.make_async_copy(dst_in, dst, sems.at[LOADS]),
            pltpu.make_async_copy(src_in, src, sems.at[LOADS + 1]),
            pltpu.make_async_copy(feats_in, feats, sems.at[LOADS + 2]),
        ]
        loads = [
            pltpu.make_async_copy(tiles_in.at[pl.ds(i * load, load)], held.at[pl.ds(i * load, load)], sems.at[i])
            for i in range(LOADS)
        ]
        for copy in copies + loads:
            copy.start()
        x_here, hi_here, core = meta[0], meta[1], meta[2]
        acc[...] = jnp.zeros_like(acc)
        copies[0].wait()
        copies[1].wait()

        def scan(i, n):
            slot = dst[i]
            near = 1 - (((slot >> 3) & 1) ^ hi_here)
            place = near * 16 + (((slot >> 4) ^ x_here) & 3) * 4 + (slot & 3)
            todo[n] = i | (src[i] << 8) | (place << 16)
            return n + (((slot >> 2) & 1) == core).astype(jnp.int32)

        ends = []
        n = jnp.int32(0)
        for i in range(LOADS):
            n = lax.fori_loop(i * load, (i + 1) * load, scan, n, unroll=8)
            ends.append(n // GROUP)
        for j in range(GROUP - 1):
            todo[n + j] = places << 16
        ends[-1] = (n + GROUP - 1) // GROUP

        def add(g, carry):
            items = [todo[g * GROUP + j] for j in range(GROUP)]
            prods = [
                jnp.dot(held[e & 255], feats[(e >> 8) & 255], preferred_element_type=jnp.float32) for e in items
            ]
            for e, prod in zip(items, prods):
                acc[e >> 16] += prod
            return carry

        copies[2].wait()
        begin = jnp.int32(0)
        for i in range(LOADS):
            loads[i].wait()
            lax.fori_loop(begin, ends[i], add, 0)
            begin = ends[i]
        out[...] = acc[:places].astype(out.dtype)

    smem = pl.BlockSpec(memory_space=pltpu.SMEM)
    hbm = pl.BlockSpec(memory_space=pltpu.HBM)
    col = lax.axis_index("col")
    meta = jnp.stack([col >> 2, (col >> 1) & 1, wanted(col & 1)]).astype(jnp.int32)
    operands = [tile_dst, tile_src, tiles, features.reshape(-1, size, width)]
    operands = [pltpu.with_memory_space_constraint(operand, pltpu.HBM) for operand in operands]
    return pl.pallas_call(
        kernel,
        out_shape=jax.ShapeDtypeStruct((places, size, width), jnp.bfloat16),
        in_specs=[smem] + [hbm] * 4,
        out_specs=pl.BlockSpec(memory_space=pltpu.VMEM),
        scratch_shapes=[
            pltpu.VMEM((places + 1, size, width), jnp.float32),
            pltpu.VMEM(tiles.shape, tiles.dtype),
            pltpu.VMEM((features.shape[0] // size, size, width), features.dtype),
            pltpu.SMEM((count,), jnp.int32),
            pltpu.SMEM((count,), jnp.int32),
            pltpu.SMEM((count + GROUP,), jnp.int32),
            pltpu.SemaphoreType.DMA((LOADS + 3,)),
        ],
        compiler_params=pltpu.CompilerParams(vmem_limit_bytes=32 * 2**20),
        cost_estimate=pl.CostEstimate(flops=32 * 2 * size * size * width, bytes_accessed=5 * 2**20, transcendentals=0),
    )(meta, *operands)


def total(parts):
    result = parts[0].astype(jnp.float32)
    for part in parts[1:]:
        result = result + part.astype(jnp.float32)
    return result


def shards(features, tiles, tile_dst, tile_src, weight, bias):
    size = tiles.shape[1]
    width = features.shape[1]
    operands = (features, tiles, tile_dst, tile_src)
    theirs = half_sums(lambda core: 1 - core, *operands)
    arrived = send(theirs, lambda x, hi, core, row: (x, hi, 1 - core, row))
    mine = half_sums(lambda core: core, *operands)

    def both(first, n):
        return total([mine[first : first + n], arrived[first : first + n]]).astype(jnp.bfloat16)

    def pieces_of(first):
        return lax.optimization_barrier([both(first + 4 * d, 4) for d in range(N_X)])

    def over_x(pieces, order):
        got = [send(pieces[d], lambda x, hi, core, row, d=d: (x ^ d, hi, core, row)) for d in order]
        return [pieces[0]] + got

    for_away = pieces_of(0)
    for_away, arrived, mine = lax.optimization_barrier((for_away, arrived, mine))
    for_home = pieces_of(16)
    away = total(over_x(for_away, (2, 3, 1))).astype(jnp.bfloat16)
    home = over_x(for_home, (3, 1, 2))
    next_row = send(away[2:], lambda x, hi, core, row: (x, 1 - hi, core, row + 1))
    same_row = send(away[:2], lambda x, hi, core, row: (x, 1 - hi, core, row))
    passed = total([part[2:] for part in home]).astype(jnp.bfloat16)
    passed = send(passed, lambda x, hi, core, row: (x, hi, core, row + 1))
    last = [part[:2] for part in home] + [same_row, next_row, passed]
    aggregate = total(last).reshape(2 * size, width)
    mixed = jnp.dot(aggregate.astype(jnp.bfloat16), weight, preferred_element_type=jnp.float32) + bias
    return jnp.maximum(mixed, 0.0).astype(jnp.bfloat16)


def solution(mesh):
    in_specs = (
        P(("col", "row"), None),
        P(("col", "row"), None, None),
        P(("col", "row")),
        P(("col", "row")),
        P(),
        P(),
    )
    out_specs = P(("col", "row"), None)
    return jax.shard_map(shards, mesh=mesh, in_specs=in_specs, out_specs=out_specs, check_vma=False)
```

```python
import jax
import jax.numpy as jnp
from jax import lax
from jax.experimental import pallas as pl
from jax.experimental.pallas import tpu as pltpu
from jax.sharding import PartitionSpec as P

N_X, N_HI, N_CORE, N_ROW = 4, 2, 2, 32
AXES = ("col", "row")
GROUP = 16
LOADS = 4


def route(move):
    pairs = []
    for c in range(N_X * N_HI * N_CORE):
        for r in range(N_ROW):
            x, hi, core, row = move(c // 4, (c // 2) % 2, c % 2, r)
            target = ((x % N_X) * 4 + hi * 2 + core) * N_ROW + row % N_ROW
            pairs.append((c * N_ROW + r, target))
    return pairs


def send(block, move):
    return lax.ppermute(block, AXES, route(move))


def half_sums(wanted, features, tiles, tile_dst, tile_src):
    count, size, _ = tiles.shape
    width = features.shape[-1]
    places = N_HI * N_X * 2 * 2
    load = count // LOADS

    def kernel(meta, dst_in, src_in, tiles_in, feats_in, out, acc, held, feats, dst, src, todo, sems):
        copies = [
            pltpu.make_async_copy(dst_in, dst, sems.at[LOADS]),
            pltpu.make_async_copy(src_in, src, sems.at[LOADS + 1]),
            pltpu.make_async_copy(feats_in, feats, sems.at[LOADS + 2]),
        ]
        loads = [
            pltpu.make_async_copy(tiles_in.at[pl.ds(i * load, load)], held.at[pl.ds(i * load, load)], sems.at[i])
            for i in range(LOADS)
        ]
        for copy in copies + loads:
            copy.start()
        x_here, hi_here, core = meta[0], meta[1], meta[2]
        acc[...] = jnp.zeros_like(acc)
        copies[0].wait()
        copies[1].wait()

        def scan(i, n):
            slot = dst[i]
            near = 1 - (((slot >> 3) & 1) ^ hi_here)
            place = near * 16 + (((slot >> 4) ^ x_here) & 3) * 4 + (slot & 3)
            todo[n] = i | (src[i] << 8) | (place << 16)
            return n + (((slot >> 2) & 1) == core).astype(jnp.int32)

        ends = []
        n = jnp.int32(0)
        for i in range(LOADS):
            n = lax.fori_loop(i * load, (i + 1) * load, scan, n, unroll=8)
            ends.append(n // GROUP)
        for j in range(GROUP - 1):
            todo[n + j] = places << 16
        ends[-1] = (n + GROUP - 1) // GROUP

        def add(g, carry):
            items = [todo[g * GROUP + j] for j in range(GROUP)]
            prods = [
                jnp.dot(held[e & 255], feats[(e >> 8) & 255], preferred_element_type=jnp.float32) for e in items
            ]
            for e, prod in zip(items, prods):
                acc[e >> 16] += prod
            return carry

        copies[2].wait()
        begin = jnp.int32(0)
        for i in range(LOADS):
            loads[i].wait()
            lax.fori_loop(begin, ends[i], add, 0)
            begin = ends[i]
        out[...] = acc[:places].astype(out.dtype)

    smem = pl.BlockSpec(memory_space=pltpu.SMEM)
    hbm = pl.BlockSpec(memory_space=pltpu.HBM)
    col = lax.axis_index("col")
    meta = jnp.stack([col >> 2, (col >> 1) & 1, wanted(col & 1)]).astype(jnp.int32)
    operands = [tile_dst, tile_src, tiles, features.reshape(-1, size, width)]
    operands = [pltpu.with_memory_space_constraint(operand, pltpu.HBM) for operand in operands]
    return pl.pallas_call(
        kernel,
        out_shape=jax.ShapeDtypeStruct((places, size, width), jnp.bfloat16),
        in_specs=[smem] + [hbm] * 4,
        out_specs=pl.BlockSpec(memory_space=pltpu.VMEM),
        scratch_shapes=[
            pltpu.VMEM((places + 1, size, width), jnp.float32),
            pltpu.VMEM(tiles.shape, tiles.dtype),
            pltpu.VMEM((features.shape[0] // size, size, width), features.dtype),
            pltpu.SMEM((count,), jnp.int32),
            pltpu.SMEM((count,), jnp.int32),
            pltpu.SMEM((count + GROUP,), jnp.int32),
            pltpu.SemaphoreType.DMA((LOADS + 3,)),
        ],
        compiler_params=pltpu.CompilerParams(vmem_limit_bytes=32 * 2**20),
        cost_estimate=pl.CostEstimate(flops=32 * 2 * size * size * width, bytes_accessed=5 * 2**20, transcendentals=0),
    )(meta, *operands)


def total(parts):
    result = parts[0].astype(jnp.float32)
    for part in parts[1:]:
        result = result + part.astype(jnp.float32)
    return result


def layer(parts, weight, bias):
    size, width = parts[0].shape[1:]

    def kernel(*refs):
        weight_ref, bias_ref, out = refs[-3:]
        summed = total([ref[:2] for ref in refs[:-3]]).reshape(2 * size, width).astype(jnp.bfloat16)
        mixed = jnp.dot(summed, weight_ref[...], preferred_element_type=jnp.float32) + bias_ref[...]
        out[...] = jnp.maximum(mixed, 0.0).astype(out.dtype)

    vmem = pl.BlockSpec(memory_space=pltpu.VMEM)
    return pl.pallas_call(
        kernel,
        out_shape=jax.ShapeDtypeStruct((2 * size, weight.shape[1]), jnp.bfloat16),
        in_specs=[vmem] * (len(parts) + 2),
        out_specs=vmem,
        compiler_params=pltpu.CompilerParams(vmem_limit_bytes=16 * 2**20),
    )(*parts, weight, bias.reshape(1, -1))


def shards(features, tiles, tile_dst, tile_src, weight, bias):
    size = tiles.shape[1]
    width = features.shape[1]
    operands = (features, tiles, tile_dst, tile_src)
    theirs = half_sums(lambda core: 1 - core, *operands)
    arrived = send(theirs, lambda x, hi, core, row: (x, hi, 1 - core, row))
    mine = half_sums(lambda core: core, *operands)

    def both(first, n):
        return total([mine[first : first + n], arrived[first : first + n]]).astype(jnp.bfloat16)

    def pieces_of(first):
        return lax.optimization_barrier([both(first + 4 * d, 4) for d in range(N_X)])

    def over_x(pieces, order):
        got = [send(pieces[d], lambda x, hi, core, row, d=d: (x ^ d, hi, core, row)) for d in order]
        return [pieces[0]] + got

    for_away = pieces_of(0)
    for_away, arrived, mine = lax.optimization_barrier((for_away, arrived, mine))
    for_home = pieces_of(16)
    away = total(over_x(for_away, (2, 3, 1))).astype(jnp.bfloat16)
    home = over_x(for_home, (3, 1, 2))
    next_row = send(away[2:], lambda x, hi, core, row: (x, 1 - hi, core, row + 1))
    same_row = send(away[:2], lambda x, hi, core, row: (x, 1 - hi, core, row))
    passed = total([part[2:] for part in home]).astype(jnp.bfloat16)
    passed = send(passed, lambda x, hi, core, row: (x, hi, core, row + 1))
    last = [*home, same_row, next_row, passed]
    return layer(last, weight, bias)


def solution(mesh):
    in_specs = (
        P(("col", "row"), None),
        P(("col", "row"), None, None),
        P(("col", "row")),
        P(("col", "row")),
        P(),
        P(),
    )
    out_specs = P(("col", "row"), None)
    return jax.shard_map(shards, mesh=mesh, in_specs=in_specs, out_specs=out_specs, check_vma=False)
```
